128 devices in a mesh: lat: 4 (over z_lo, core), lon: 32 (over x, y, z_hi).
Axes of the slice: x: 4, y: 4, z: 4 (z_hi: 2, z_lo: 2; z = z_hi * 2 + z_lo), core: 2. Of those that a mesh axis runs over, the one named last changes fastest.
Arguments:
- field: bfloat16 [512, 1024, 256], P('lat', 'lon'), may hold values from -6 to 6
- norm_gain: float32 [256], replicated, may hold values from 0.1 to 1.9
- expand_weight: bfloat16 [256, 1024], replicated, may hold values from -0.375 to 0.375
- expand_bias: float32 [1024], replicated, may hold values from -3 to 3
- depth_kernel: float32 [3, 3, 1024], replicated, may hold values from -2 to 2
- depth_bias: float32 [1024], replicated, may hold values from -3 to 3
- project_weight: bfloat16 [1024, 256], replicated, may hold values from -0.1875 to 0.1875
- block_gain: float32 [256], replicated, may hold values from 0.1 to 1.9
- block_qkv: bfloat16 [256, 768], replicated, may hold values from -0.375 to 0.375
- block_out: bfloat16 [256, 256], replicated, may hold values from -0.375 to 0.375
- grid_gain: float32 [256], replicated, may hold values from 0.1 to 1.9
- grid_qkv: bfloat16 [256, 768], replicated, may hold values from -0.375 to 0.375
- grid_out: bfloat16 [256, 256], replicated, may hold values from -0.375 to 0.375
Outputs:
- result: bfloat16 [512, 1024, 256], P('lat', 'lon')
The draws below stay inside these ranges and needn't reach their ends.
All inputs are finite; a program needn't handle non-finite values.
Results may differ from the reference program's by a relative error of at most 0.012.
Values may be sent and summed in bfloat16 or wider, within the bound.
No kernel may reach another device: no remote copies, remote signals or barrier semaphores. Data moves between devices by JAX's collectives and lax.ppermute only.
A program may use at most 128 MiB of HBM per device.

```python
import jax
import jax.numpy as jnp
from jax import lax

C = 256
HEADS = 8
EXPANDED = 1024
LAT_CELLS = 512
LON_CELLS = 1024


def shard_levels(key, dims, pieces, smallest, largest):
    def one(axis_at, parts):
        steps = jax.random.uniform(jax.random.fold_in(jax.random.fold_in(key, 6), axis_at), (parts,), jnp.float32, smallest / len(pieces), largest / len(pieces))
        return jnp.repeat(jnp.exp(steps), dims[axis_at] // parts).reshape((-1,) + (1,) * (len(dims) - axis_at - 1))

    level = one(*pieces[0])
    for cut in pieces[1:]:
        level = level * one(*cut)
    return level


def bell_draw(stream_key, shape, scale, limit, cuts=(), held_as=jnp.bfloat16):
    entries = jax.random.normal(stream_key, shape, jnp.float32) * scale
    if len(cuts) > 0:
        entries = shard_levels(stream_key, shape, cuts, -0.22, 0.18) * entries
    return jnp.clip(entries, min=-limit, max=limit).astype(held_as)


def setup_inputs(seed: int = 0) -> dict:
    arg_keys = jax.random.split(jax.random.key(seed), 14)
    return {
        "field": bell_draw(arg_keys[0], (LAT_CELLS, LON_CELLS, C), 1.0, 6.0, ((0, 4), (1, 32))),
        "norm_gain": jnp.clip(1.0 + 0.18 * jax.random.normal(arg_keys[1], (C,), jnp.float32), 0.1, 1.9),
        "expand_weight": bell_draw(arg_keys[2], (C, EXPANDED), C ** -0.5, 0.375),
        "expand_bias": bell_draw(arg_keys[3], (EXPANDED,), 0.5, 3.0, (), jnp.float32),
        "depth_kernel": bell_draw(arg_keys[4], (3, 3, EXPANDED), 9 ** -0.5, 2.0, (), jnp.float32),
        "depth_bias": bell_draw(arg_keys[5], (EXPANDED,), 0.5, 3.0, (), jnp.float32),
        "project_weight": bell_draw(arg_keys[6], (EXPANDED, C), EXPANDED ** -0.5, 0.1875),
        "block_gain": jnp.clip(1.0 + 0.18 * jax.random.normal(arg_keys[7], (C,), jnp.float32), 0.1, 1.9),
        "block_qkv": bell_draw(arg_keys[8], (C, 3 * C), C ** -0.5, 0.375),
        "block_out": bell_draw(arg_keys[9], (C, C), C ** -0.5, 0.375),
        "grid_gain": jnp.clip(1.0 + 0.18 * jax.random.normal(arg_keys[10], (C,), jnp.float32), 0.1, 1.9),
        "grid_qkv": bell_draw(arg_keys[11], (C, 3 * C), C ** -0.5, 0.375),
        "grid_out": bell_draw(arg_keys[12], (C, C), C ** -0.5, 0.375),
    }


def norm_rows(values, gain):
    mean = lax.optimization_barrier(jnp.mean(values, axis=-1, keepdims=True))
    centred = values - mean
    var = lax.optimization_barrier(jnp.mean(centred * centred, axis=-1, keepdims=True))
    return centred * lax.rsqrt(var + 1e-05) * gain

def attend(tokens, gain, w_qkv, w_out):
    count, group, width = tokens.shape
    head_size = width // HEADS
    normed = norm_rows(tokens.astype(jnp.float32), gain).astype(jnp.bfloat16)
    packed = jnp.dot(normed.reshape(-1, width), w_qkv, preferred_element_type=jnp.float32).astype(jnp.bfloat16)
    packed = packed.reshape(count, group, 3, HEADS, head_size).astype(jnp.float32)
    query = packed[:, :, 0]
    keys = packed[:, :, 1]
    values = packed[:, :, 2]
    scores = jnp.einsum('nqhd,nkhd->nhqk', query, keys) * head_size ** (-0.5)
    weights = jax.nn.softmax(scores, axis=-1).astype(jnp.bfloat16).astype(jnp.float32)
    mixed = jnp.einsum('nhqk,nkhd->nqhd', weights, values).astype(jnp.bfloat16)
    added = jnp.dot(mixed.reshape(-1, width), w_out, preferred_element_type=jnp.float32)
    return (tokens.astype(jnp.float32) + added.reshape(count, group, width)).astype(jnp.bfloat16)

def reference(field, norm_gain, expand_weight, expand_bias, depth_kernel, depth_bias, project_weight, block_gain, block_qkv, block_out, grid_gain, grid_qkv, grid_out):
    rows_all, cols_all, width = field.shape
    wide = expand_weight.shape[1]
    normed = norm_rows(field.astype(jnp.float32), norm_gain).astype(jnp.bfloat16)
    padded = jnp.pad(normed, ((1, 1), (1, 1), (0, 0)))
    band = 8
    col_index = jnp.arange(cols_all + 2, dtype=jnp.int32)
    col_valid = (col_index >= 1) & (col_index <= cols_all)

    def bottleneck(band_index):
        start = (band_index * band).astype(jnp.int32)
        piece = lax.dynamic_slice_in_dim(padded, start, band + 2, 0)
        grown = jnp.dot(piece.reshape(-1, width), expand_weight, preferred_element_type=jnp.float32) + expand_bias
        grown = jax.nn.gelu(grown, approximate=True).reshape(band + 2, cols_all + 2, wide)
        row_index = start + jnp.arange(band + 2, dtype=jnp.int32)
        valid = ((row_index >= 1) & (row_index <= rows_all))[:, None] & col_valid[None, :]
        grown = jnp.where(valid[:, :, None], grown, 0.0).astype(jnp.bfloat16).astype(jnp.float32)
        total = jnp.zeros((band, cols_all, wide), jnp.float32) + depth_bias
        for shift_r in range(3):
            for shift_c in range(3):
                total = total + depth_kernel[shift_r, shift_c] * grown[shift_r:shift_r + band, shift_c:shift_c + cols_all]
        filtered = jax.nn.gelu(total, approximate=True).astype(jnp.bfloat16)
        added = jnp.dot(filtered.reshape(-1, wide), project_weight, preferred_element_type=jnp.float32)
        own = lax.dynamic_slice_in_dim(field, start, band, 0).astype(jnp.float32)
        return (own + added.reshape(band, cols_all, width)).astype(jnp.bfloat16)
    mixed = lax.map(bottleneck, jnp.arange(rows_all // band, dtype=jnp.int32)).reshape(rows_all, cols_all, width)
    windows = mixed.reshape(rows_all // 8, 8, cols_all // 8, 8, width).transpose(0, 2, 1, 3, 4)
    windows = windows.reshape(rows_all // 8, cols_all // 8, 64, width)
    windows = lax.map(lambda row: attend(row, block_gain, block_qkv, block_out), windows)
    blocked = windows.reshape(rows_all // 8, cols_all // 8, 8, 8, width).transpose(0, 2, 1, 3, 4).reshape(rows_all, cols_all, width)
    stride_r = rows_all // 8
    stride_c = cols_all // 8
    groups = blocked.reshape(8, stride_r, 8, stride_c, width).transpose(1, 3, 0, 2, 4).reshape(stride_r, stride_c, 64, width)
    groups = lax.map(lambda row: attend(row, grid_gain, grid_qkv, grid_out), groups)
    result = groups.reshape(stride_r, stride_c, 8, 8, width).transpose(2, 0, 3, 1, 4).reshape(rows_all, cols_all, width)
    return result
```

```python
import functools
import math

import jax
import jax.numpy as jnp
from jax import lax
from jax.experimental import pallas as pl
from jax.experimental.pallas import tpu as pltpu
from jax.sharding import Mesh
from jax.sharding import PartitionSpec as P

HEADS = 8
WIDTH = 256
HEAD = WIDTH // HEADS
WIDE = 1024
COLS = 32
SLICE = 256
PARTS = 2
F32 = jnp.float32
BF16 = jnp.bfloat16
VMEM_LIMIT = 56 * 1024 * 1024


def norm_rows(values, gain):
    mean = jnp.mean(values, axis=-1, keepdims=True)
    centred = values - mean
    var = jnp.mean(centred * centred, axis=-1, keepdims=True)
    return centred * lax.rsqrt(var + 1e-05) * gain


def double_gelu(x):
    inner = x * (0.7978845608028654 + (0.7978845608028654 * 0.044715) * (x * x))
    return x + x * jnp.tanh(inner)


def attend(tokens, gain, w_qv_t, w_k, w_out):
    normed = norm_rows(tokens, gain).astype(BF16)
    qv = lax.dot_general(w_qv_t, normed, (((1,), (1,)), ((), ())), preferred_element_type=F32)
    scale = HEAD ** -0.5 * math.log2(math.e)
    q_t = (qv[:WIDTH] * scale).astype(BF16)
    v_t = qv[WIDTH:].astype(BF16)
    keys = jnp.dot(normed, w_k, preferred_element_type=F32).astype(BF16)
    low = lax.broadcasted_iota(jnp.int32, (HEAD, 128), 1) < 64
    zero_q = jnp.zeros((64, 128), BF16)
    zero_p = jnp.zeros((64, 128), BF16)
    none = jnp.zeros((HEAD, 128), BF16)
    outs = []
    for a in range(2):
        here = q_t[:, 128 * a : 128 * (a + 1)]
        over = jnp.concatenate([here[:, 64:], here[:, :64]], axis=1)
        probs = []
        inverse = []
        for g in range(2):
            straight, crossed = (here, over) if g == 0 else (over, here)
            row0 = 128 * a + 64 * g
            for t in range(2):
                pair = []
                for jj in range(2):
                    at = 128 * t + 64 * jj
                    first = jnp.where(low, straight[at : at + HEAD], none)
                    second = jnp.where(low, none, crossed[at + HEAD : at + 64])
                    pair.append(jnp.concatenate([first, second], axis=0))
                rhs = jnp.concatenate(
                    [
                        jnp.concatenate([pair[0], zero_q], axis=1),
                        jnp.concatenate([zero_q, pair[1]], axis=1),
                    ],
                    axis=0,
                )
                scores = jnp.dot(
                    keys[row0 : row0 + 64, 128 * t : 128 * (t + 1)], rhs, preferred_element_type=F32
                )
                top = jnp.max(scores, axis=0, keepdims=True)
                weights = jnp.exp2(scores - top)
                total = jnp.sum(weights, axis=0, keepdims=True)
                probs.append(weights.astype(BF16))
                inverse.append(1.0 / total)
        for j in range(4):
            t, jj = j // 2, j % 2
            lanes = slice(128 * jj, 128 * (jj + 1))
            p0, p1 = probs[t][:, lanes], probs[2 + t][:, lanes]
            rhs = jnp.concatenate(
                [jnp.concatenate([p0, zero_p], axis=1), jnp.concatenate([zero_p, p1], axis=1)], axis=0
            )
            out = jnp.dot(
                v_t[64 * j : 64 * (j + 1), 128 * a : 128 * (a + 1)], rhs, preferred_element_type=F32
            )
            o0 = out[:, :128] * inverse[t][:, lanes]
            o1 = out[:, 128:] * inverse[2 + t][:, lanes]
            r0 = pltpu.roll(o0[HEAD:], 64, 1)
            r1 = pltpu.roll(o1[:HEAD], 64, 1)
            outs.append((a, jnp.where(low, o0[:HEAD], r1).astype(BF16)))
            outs.append((a, jnp.where(low, r0, o1[HEAD:]).astype(BF16)))
    mixed_t = jnp.concatenate(
        [jnp.concatenate([o for a, o in outs if a == half], axis=0) for half in range(2)], axis=1
    )
    added = lax.dot_general(mixed_t, w_out, (((0,), (0,)), ((), ())), preferred_element_type=F32)
    return tokens + added


def local_kernel(
    part,
    flags_ref,
    main_ref,
    above_ref,
    below_ref,
    north_ref,
    south_ref,
    side_ref,
    gain_ref,
    w_expand_ref,
    b_expand_ref,
    depth_ref,
    b_depth_ref,
    w_project_ref,
    gain2_ref,
    w_qv_ref,
    w_k_ref,
    w_out_ref,
    out_ref,
):
    per = 8 // PARTS
    band = pl.program_id(0) * 8 + part * per + pl.program_id(1)
    is_first = band == 0
    is_last = band == 15
    own = main_ref[...].astype(F32)
    top = jnp.where(is_first, north_ref[...].astype(F32), above_ref[...].astype(F32))
    bottom = jnp.where(is_last, south_ref[...].astype(F32), below_ref[...].astype(F32))
    top_keep = jnp.where(is_first, flags_ref[0], 1.0)
    bottom_keep = jnp.where(is_last, flags_ref[1], 1.0)
    left_keep, right_keep = flags_ref[2], flags_ref[3]
    cells = jnp.concatenate(
        [
            top.reshape(COLS, WIDTH),
            own.reshape(8 * COLS, WIDTH),
            bottom.reshape(COLS, WIDTH),
            side_ref[0].astype(F32),
        ],
        axis=0,
    )
    normed = norm_rows(cells, gain_ref[...]).astype(BF16)
    col = lax.broadcasted_iota(jnp.int32, (COLS, SLICE), 0)
    at_left = col == 0
    at_right = col == COLS - 1
    side_row = lax.broadcasted_iota(jnp.int32, (16, SLICE), 0)
    side_edge = jnp.where(side_row == 0, top_keep, jnp.where(side_row == 9, bottom_keep, 1.0))
    acc = own.reshape(8 * COLS, WIDTH)
    for s in range(WIDE // SLICE):
        lanes = slice(s * SLICE, (s + 1) * SLICE)
        grown = jnp.dot(normed, w_expand_ref[:, lanes], preferred_element_type=F32)
        grown = double_gelu(grown + b_expand_ref[:, lanes])
        rows = [grown[COLS * i : COLS * (i + 1)] for i in range(10)]
        rows[0] = rows[0] * top_keep
        rows[9] = rows[9] * bottom_keep
        rows = [r.astype(BF16).astype(F32) for r in rows]
        left = (grown[10 * COLS : 10 * COLS + 16] * (side_edge * left_keep)).astype(BF16).astype(F32)
        right = (grown[10 * COLS + 16 :] * (side_edge * right_keep)).astype(BF16).astype(F32)
        taps = [[depth_ref[3 * di + dj : 3 * di + dj + 1, lanes] for dj in range(3)] for di in range(3)]
        left = sum(taps[di][0] * left[di : di + 8] for di in range(3))
        right = sum(taps[di][2] * right[di : di + 8] for di in range(3))
        pieces = []
        for r in range(8):
            p = [
                taps[0][dj] * rows[r] + taps[1][dj] * rows[r + 1] + taps[2][dj] * rows[r + 2]
                for dj in range(3)
            ]
            from_left = jnp.where(at_left, left[r : r + 1], pltpu.roll(p[0], 1, 0))
            from_right = jnp.where(at_right, right[r : r + 1], pltpu.roll(p[2], COLS - 1, 0))
            total = (p[1] + b_depth_ref[:, lanes]) + (from_left + from_right)
            pieces.append(double_gelu(total).astype(BF16))
        filtered = jnp.concatenate(pieces, axis=0)
        acc = acc + jnp.dot(filtered, w_project_ref[lanes, :], preferred_element_type=F32)
    mixed = acc.astype(BF16).astype(F32)
    tokens = jnp.concatenate(
        [
            mixed[COLS * r + 8 * b : COLS * r + 8 * b + 8]
            for b in range(4)
            for r in range(8)
        ],
        axis=0,
    )
    done = attend(tokens, gain2_ref[...], w_qv_ref[...], w_k_ref[...], w_out_ref[...])
    done = jnp.concatenate(
        [done[64 * b + 8 * r : 64 * b + 8 * r + 8] for r in range(8) for b in range(4)], axis=0
    )
    out_ref[...] = done.astype(BF16).reshape(8, 1, COLS, WIDTH)


def local_stage(part, flags, field, north, south, side, weights):
    per = 8 // PARTS
    band = lambda i, r: i * 8 + part * per + r
    whole = lambda a: pl.BlockSpec(a.shape, lambda i, r: (0,) * a.ndim)
    return pl.pallas_call(
        functools.partial(local_kernel, part),
        grid=(2, per),
        in_specs=[
            pl.BlockSpec(memory_space=pltpu.SMEM),
            pl.BlockSpec((8, COLS, WIDTH), lambda i, r: (band(i, r), 0, 0)),
            pl.BlockSpec((1, COLS, WIDTH), lambda i, r: (jnp.maximum(band(i, r) * 8 - 1, 0), 0, 0)),
            pl.BlockSpec((1, COLS, WIDTH), lambda i, r: (jnp.minimum(band(i, r) * 8 + 8, 127), 0, 0)),
            whole(north),
            whole(south),
            pl.BlockSpec((1, COLS, WIDTH), lambda i, r: (band(i, r), 0, 0)),
        ]
        + [whole(w) for w in weights],
        out_specs=pl.BlockSpec((8, 1, COLS, WIDTH), lambda i, r: (r, i, 0, 0)),
        out_shape=jax.ShapeDtypeStruct((8 * per, 2, COLS, WIDTH), BF16),
        compiler_params=pltpu.CompilerParams(
            dimension_semantics=("arbitrary", "arbitrary"), vmem_limit_bytes=VMEM_LIMIT
        ),
        cost_estimate=pl.CostEstimate(
            flops=10_000_000_000 // PARTS, bytes_accessed=6_000_000 // PARTS, transcendentals=12_000_000 // PARTS
        ),
        name="local_stage",
    )(flags, field, field, field, north, south, side, *weights)


def grid_kernel(in_ref, gain_ref, w_qv_ref, w_k_ref, w_out_ref, out_ref):
    i = lax.broadcasted_iota(jnp.int32, (256, 256), 0)
    j = lax.broadcasted_iota(jnp.int32, (256, 256), 1)
    swap = jnp.where((i % 16) * 16 + i // 16 == j, 1.0, 0.0).astype(BF16)
    turned = []
    for c in range(4):
        block = in_ref[8 * c : 8 * c + 8].reshape(256, WIDTH)
        turned.append(jnp.dot(swap, block, preferred_element_type=F32))
    done = []
    for g in range(4):
        tokens = jnp.concatenate(
            [turned[c][64 * g + 16 * k : 64 * g + 16 * k + 16] for k in range(4) for c in range(4)], axis=0
        )
        done.append(
            attend(tokens, gain_ref[...], w_qv_ref[...], w_k_ref[...], w_out_ref[...]).astype(BF16)
        )
    for c in range(4):
        block = jnp.concatenate(
            [done[g][64 * k + 16 * c : 64 * k + 16 * c + 16] for g in range(4) for k in range(4)], axis=0
        )
        back = jnp.dot(swap, block, preferred_element_type=F32).astype(BF16)
        out_ref[8 * c : 8 * c + 8] = back.reshape(8, 1, 2, 16, WIDTH)


def grid_stage(landed, weights):
    rows = landed.shape[1]
    whole = lambda a: pl.BlockSpec(a.shape, lambda r, h: (0,) * a.ndim)
    block = pl.BlockSpec((32, 1, 2, 16, WIDTH), lambda r, h: (0, r, 0, h, 0))
    return pl.pallas_call(
        grid_kernel,
        grid=(rows, 2),
        in_specs=[block] + [whole(w) for w in weights],
        out_specs=block,
        out_shape=jax.ShapeDtypeStruct(landed.shape, BF16),
        compiler_params=pltpu.CompilerParams(
            dimension_semantics=("arbitrary", "arbitrary"), vmem_limit_bytes=VMEM_LIMIT
        ),
        cost_estimate=pl.CostEstimate(
            flops=6_000_000_000 // PARTS, bytes_accessed=5_000_000 // PARTS, transcendentals=2_000_000 // PARTS
        ),
        name="grid_stage",
    )(landed, *weights)


def shift(values, axis, step, count):
    pairs = [(i, i + step) for i in range(count) if 0 <= i + step < count]
    return lax.ppermute(values, axis, pairs)


LON = ("j", "m")


def per_device(
    field,
    norm_gain,
    expand_weight,
    expand_bias,
    depth_kernel,
    depth_bias,
    project_weight,
    block_gain,
    block_qkv,
    block_out,
    grid_gain,
    grid_qkv,
    grid_out,
):
    lat_count, lon_count = 4, 32
    north = shift(field[-1:], "lat", 1, lat_count)
    south = shift(field[:1], "lat", -1, lat_count)

    def side(at):
        return jnp.concatenate([north[:, at], field[:, at], south[:, at]], axis=0)

    left = shift(side(COLS - 1), LON, 1, lon_count)
    right = shift(side(0), LON, -1, lon_count)

    def windows(column):
        column = jnp.pad(column, ((0, 6), (0, 0))).reshape(17, 8, WIDTH)
        return jnp.concatenate([column[:16], column[1:]], axis=1)

    sides = jnp.concatenate([windows(left), windows(right)], axis=1)
    lat = lax.axis_index("lat")
    lon = lax.axis_index(LON)
    flags = jnp.stack([lat > 0, lat < lat_count - 1, lon > 0, lon < lon_count - 1]).astype(F32)

    def attend_weights(gain, qkv, out):
        q, k, v = qkv[:, :WIDTH], qkv[:, WIDTH : 2 * WIDTH], qkv[:, 2 * WIDTH :]
        return (gain[None], jnp.concatenate([q, v], axis=1).T, k, out)

    local_weights = (
        norm_gain[None],
        expand_weight,
        expand_bias[None],
        0.5 * depth_kernel.reshape(9, WIDE),
        depth_bias[None],
        (0.5 * project_weight.astype(F32)).astype(BF16),
    ) + attend_weights(block_gain, block_qkv, block_out)
    grid_weights = attend_weights(grid_gain, grid_qkv, grid_out)
    per_dest = 2 // PARTS
    landed = []
    for part in range(PARTS):
        parcels = local_stage(part, flags, field, north, south, sides, local_weights)
        parcels = parcels.reshape(32, per_dest * 2 * COLS, WIDTH)
        landed.append(lax.all_to_all(parcels, ("lat", "j"), 0, 0, tiled=True))
    results = []
    for part in range(PARTS):
        groups = landed[part].reshape(32, per_dest, 2, COLS, WIDTH)
        groups = grid_stage(groups, grid_weights)
        back = lax.all_to_all(groups.reshape(32, per_dest * 2 * COLS, WIDTH), ("lat", "j"), 0, 0, tiled=True)
        results.append(back.reshape(64 // PARTS, 2, COLS, WIDTH).transpose(1, 0, 2, 3))
    return jnp.concatenate(results, axis=1).reshape(128, COLS, WIDTH)


def solution(mesh):
    inner = Mesh(mesh.devices.reshape(4, 8, 4), ("lat", "j", "m"))
    return jax.shard_map(
        per_device,
        mesh=inner,
        in_specs=(P("lat", LON, None),) + (P(),) * 12,
        out_specs=P("lat", LON, None),
        check_vma=False,
    )
```

```python
import functools
import math

import jax
import jax.numpy as jnp
from jax import lax
from jax.experimental import pallas as pl
from jax.experimental.pallas import tpu as pltpu
from jax.sharding import Mesh
from jax.sharding import PartitionSpec as P

HEADS = 8
WIDTH = 256
HEAD = WIDTH // HEADS
WIDE = 1024
COLS = 32
SLICE = 256
F32 = jnp.float32
BF16 = jnp.bfloat16
VMEM_LIMIT = 56 * 1024 * 1024


def norm_rows(values, gain):
    mean = jnp.mean(values, axis=-1, keepdims=True)
    centred = values - mean
    var = jnp.mean(centred * centred, axis=-1, keepdims=True)
    return centred * lax.rsqrt(var + 1e-05) * gain


def double_gelu(x):
    c0 = jnp.asarray(0.7978845608028654, x.dtype)
    c1 = jnp.asarray(0.7978845608028654 * 0.044715, x.dtype)
    return x + x * jnp.tanh(x * (c0 + c1 * (x * x)))


def swap_matrix():
    i = lax.broadcasted_iota(jnp.int32, (256, 256), 0)
    j = lax.broadcasted_iota(jnp.int32, (256, 256), 1)
    return jnp.where((i % 16) * 16 + i // 16 == j, 1.0, 0.0).astype(BF16)


def attend(tokens, gain, w_qkv, w_out):
    count = tokens.shape[0]
    normed = norm_rows(tokens, gain).astype(BF16)
    scale = HEAD ** -0.5 * math.log2(math.e)
    w_qv_t = jnp.concatenate([w_qkv[:, :WIDTH], w_qkv[:, 2 * WIDTH :]], axis=1).T
    keys = jnp.dot(normed, w_qkv[:, WIDTH : 2 * WIDTH], preferred_element_type=F32).astype(BF16)
    low = lax.broadcasted_iota(jnp.int32, (HEAD, 128), 1) < 64
    zero = jnp.zeros((64, 128), BF16)
    none = jnp.zeros((HEAD, 128), BF16)
    q_t, v_t = [], []
    for i in range(count // 256):
        qv = lax.dot_general(
            w_qv_t,
            normed[256 * i : 256 * (i + 1)],
            (((1,), (1,)), ((), ())),
            preferred_element_type=F32,
        )
        q_t += [(qv[:WIDTH, 128 * a : 128 * (a + 1)] * scale).astype(BF16) for a in range(2)]
        v_t += [qv[WIDTH:, 128 * a : 128 * (a + 1)].astype(BF16) for a in range(2)]
    scores = {}
    for n, here in enumerate(q_t):
        over = jnp.concatenate([here[:, 64:], here[:, :64]], axis=1)
        for g in range(2):
            straight, crossed = (here, over) if g == 0 else (over, here)
            row0 = 128 * n + 64 * g
            for t in range(2):
                pair = []
                for jj in range(2):
                    at = 128 * t + 64 * jj
                    first = jnp.where(low, straight[at : at + HEAD], none)
                    second = jnp.where(low, none, crossed[at + HEAD : at + 64])
                    pair.append(jnp.concatenate([first, second], axis=0))
                rhs = jnp.concatenate(
                    [
                        jnp.concatenate([pair[0], zero], axis=1),
                        jnp.concatenate([zero, pair[1]], axis=1),
                    ],
                    axis=0,
                )
                scores[n, g, t] = jnp.dot(
                    keys[row0 : row0 + 64, 128 * t : 128 * (t + 1)], rhs, preferred_element_type=F32
                )
    probs, inverse = {}, {}
    for at, score in scores.items():
        weights = jnp.exp2(score - jnp.max(score, axis=0, keepdims=True))
        inverse[at] = 1.0 / jnp.sum(weights, axis=0, keepdims=True)
        probs[at] = weights.astype(BF16)
    raw = {}
    for n in range(count // 128):
        for j in range(4):
            t, jj = j // 2, j % 2
            lanes = slice(128 * jj, 128 * (jj + 1))
            p0, p1 = probs[n, 0, t][:, lanes], probs[n, 1, t][:, lanes]
            rhs = jnp.concatenate(
                [jnp.concatenate([p0, zero], axis=1), jnp.concatenate([zero, p1], axis=1)], axis=0
            )
            raw[n, j] = jnp.dot(v_t[n][64 * j : 64 * (j + 1)], rhs, preferred_element_type=F32)
    mixed = []
    for n in range(count // 128):
        outs = []
        for j in range(4):
            t, jj = j // 2, j % 2
            lanes = slice(128 * jj, 128 * (jj + 1))
            o0 = raw[n, j][:, :128] * inverse[n, 0, t][:, lanes]
            o1 = raw[n, j][:, 128:] * inverse[n, 1, t][:, lanes]
            outs.append(jnp.where(low, o0[:HEAD], pltpu.roll(o1[:HEAD], 64, 1)).astype(BF16))
            outs.append(jnp.where(low, pltpu.roll(o0[HEAD:], 64, 1), o1[HEAD:]).astype(BF16))
        mixed.append(jnp.concatenate(outs, axis=0).T)
    mixed = jnp.concatenate(mixed, axis=0)
    return tokens + jnp.dot(mixed, w_out, preferred_element_type=F32)


def local_kernel(
    blocks,
    field_ref,
    north_ref,
    south_ref,
    *refs,
):
    edge = 0 in blocks
    if edge:
        side_ref, refs = refs[0], refs[1:]
    (
        gain_ref,
        w_expand_ref,
        b_expand_ref,
        depth_ref,
        b_depth_ref,
        w_project_ref,
        gain2_ref,
        w_qkv_ref,
        w_out_ref,
        out_ref,
        normed_ref,
        grown_ref,
        filtered_ref,
        acc_ref,
    ) = refs
    row = lax.broadcasted_iota(jnp.int32, (160, 512), 0)
    lane = lax.broadcasted_iota(jnp.int32, (160, 512), 1)
    same_band = row % 16 == lane // COLS
    col_gap = lane % COLS - row // 16
    k_of = lax.broadcasted_iota(jnp.int32, (160, SLICE), 0) % 16
    lat = lax.axis_index("lat")
    lon = lax.axis_index("j") * lax.axis_size("m") + lax.axis_index("m")
    keep_left = jnp.where(lon == 0, 0.0, 1.0)
    keep_right = jnp.where(lon == 8 * lax.axis_size("m") - 1, 0.0, 1.0)
    keep_top = jnp.where((k_of == 0) & (lat == 0), 0.0, 1.0).astype(BF16)
    keep_bottom = jnp.where((k_of == 15) & (lat == 3), 0.0, 1.0).astype(BF16)
    swap = swap_matrix()
    halves = []
    for block in blocks:
        window = 8 * block - 1
        pick = jnp.where(same_band & (col_gap == window), 1.0, 0.0).astype(BF16)
        on_side = block == 0 or block == COLS // 8 - 1
        if on_side:
            srow = lax.broadcasted_iota(jnp.int32, (160, 32), 0)
            slane = lax.broadcasted_iota(jnp.int32, (160, 32), 1)
            column = 0 if block == 0 else 9
            lane0 = 0 if block == 0 else 16
            pick_side = jnp.where(
                (srow // 16 == column) & (srow % 16 + lane0 == slane), 1.0, 0.0
            ).astype(BF16)
        for r in range(10):
            if r == 0:
                rows = jnp.concatenate(
                    [north_ref[...]] + [field_ref[8 * k + 7 : 8 * k + 8] for k in range(15)], axis=0
                )
            elif r == 9:
                rows = jnp.concatenate(
                    [field_ref[8 * k : 8 * k + 1] for k in range(1, 16)] + [south_ref[...]], axis=0
                )
            else:
                rows = jnp.concatenate(
                    [field_ref[8 * k + r - 1 : 8 * k + r] for k in range(16)], axis=0
                )
            cells = jnp.dot(pick, rows.reshape(512, WIDTH), preferred_element_type=F32)
            if on_side:
                cells = cells + jnp.dot(pick_side, side_ref[r], preferred_element_type=F32)
            if 1 <= r <= 8:
                acc_ref[128 * (r - 1) : 128 * r] = cells[16:144]
            normed_ref[160 * r : 160 * (r + 1)] = norm_rows(cells, gain_ref[...]).astype(BF16)

        def channels(s, _):
            at = pl.ds(pl.multiple_of(s * SLICE, SLICE), SLICE)
            bias = jnp.broadcast_to(b_expand_ref[:, at], (16, SLICE)).astype(BF16)
            bias = jnp.concatenate([bias] * 10, axis=0)
            w_here = w_expand_ref[:, at]
            grown = jnp.dot(normed_ref[...], w_here, preferred_element_type=F32).astype(BF16)
            for r in range(10):
                g = double_gelu(grown[160 * r : 160 * (r + 1)] + bias)
                if r == 0:
                    g = g * keep_top
                if r == 9:
                    g = g * keep_bottom
                if on_side:
                    keep = keep_left if block == 0 else keep_right
                    if block == 0:
                        g = jnp.concatenate([(g[:16] * keep.astype(BF16)), g[16:]], axis=0)
                    else:
                        g = jnp.concatenate([g[:144], (g[144:] * keep.astype(BF16))], axis=0)
                grown_ref[r] = g.reshape(10, 16, SLICE)
            for half in range(SLICE // 128):
                lanes = slice(128 * half, 128 * (half + 1))
                there = pl.ds(pl.multiple_of(s * SLICE + 128 * half, 128), 128)
                taps = [
                    jnp.broadcast_to(0.5 * depth_ref[i : i + 1, there], (16, 128)).astype(BF16)
                    for i in range(9)
                ]
                depth_bias = jnp.broadcast_to(b_depth_ref[:, there], (16, 128)).astype(BF16)
                for c in range(8):
                    near = [[grown_ref[r, c + dj, :, lanes] for r in range(10)] for dj in range(3)]
                    for r in range(8):
                        p = [
                            taps[dj] * near[dj][r]
                            + taps[3 + dj] * near[dj][r + 1]
                            + taps[6 + dj] * near[dj][r + 2]
                            for dj in range(3)
                        ]
                        total = (p[0] + p[1]) + (p[2] + depth_bias)
                        filtered_ref[r, c, :, lanes] = double_gelu(total)
            acc_ref[...] += jnp.dot(
                filtered_ref[...].reshape(1024, SLICE),
                w_project_ref[at, :] * jnp.asarray(0.5, BF16),
                preferred_element_type=F32,
            )
            return 0

        lax.fori_loop(0, WIDE // SLICE, channels, 0)
        mixed = acc_ref[...].astype(BF16)
        turned = [
            jnp.dot(swap, mixed[256 * i : 256 * (i + 1)], preferred_element_type=F32) for i in range(4)
        ]
        tokens = jnp.concatenate(
            [turned[i][16 * k : 16 * k + 16] for k in range(16) for i in range(4)], axis=0
        )
        halves.append(attend(tokens, gain2_ref[...], w_qkv_ref[...], w_out_ref[...]))
    for k in range(16):
        both = jnp.concatenate(
            [halves[h][64 * k : 64 * k + 64].reshape(8, 8, WIDTH) for h in range(2)], axis=1
        )
        out_ref[8 * (k % 8) : 8 * (k % 8) + 8, k // 8] = both.astype(BF16)


def local_stage(blocks, field, north, south, side, weights):
    vmem = pl.BlockSpec(memory_space=pltpu.VMEM)
    arrays = (field, north, south) + ((side,) if 0 in blocks else ()) + weights
    return pl.pallas_call(
        functools.partial(local_kernel, blocks),
        in_specs=[vmem] * len(arrays),
        out_specs=vmem,
        out_shape=jax.ShapeDtypeStruct((64, 2, 16, WIDTH), BF16),
        scratch_shapes=[
            pltpu.VMEM((1600, WIDTH), BF16),
            pltpu.VMEM((10, 10, 16, SLICE), BF16),
            pltpu.VMEM((8, 8, 16, SLICE), BF16),
            pltpu.VMEM((1024, WIDTH), F32),
        ],
        compiler_params=pltpu.CompilerParams(vmem_limit_bytes=VMEM_LIMIT),
        cost_estimate=pl.CostEstimate(
            flops=5_000_000_000, bytes_accessed=3_000_000, transcendentals=6_000_000
        ),
        name="local_stage",
    )(*arrays)


def grid_kernel(in_ref, gain_ref, w_qkv_ref, w_out_ref, out_ref):
    swap = swap_matrix()
    turned = []
    for c in range(4):
        block = in_ref[8 * c : 8 * c + 8].reshape(256, WIDTH)
        turned.append(jnp.dot(swap, block, preferred_element_type=F32))
    tokens = jnp.concatenate(
        [turned[c][16 * k : 16 * k + 16] for k in range(16) for c in range(4)], axis=0
    )
    done = attend(tokens, gain_ref[...], w_qkv_ref[...], w_out_ref[...]).astype(BF16)
    for c in range(4):
        block = jnp.concatenate([done[64 * k + 16 * c : 64 * k + 16 * c + 16] for k in range(16)], axis=0)
        back = jnp.dot(swap, block, preferred_element_type=F32).astype(BF16)
        out_ref[8 * c : 8 * c + 8] = back.reshape(8, 1, 2, 16, WIDTH)


def grid_stage(landed, weights):
    rows = landed.shape[1]
    whole = lambda a: pl.BlockSpec(a.shape, lambda r: (0,) * a.ndim)
    block = pl.BlockSpec((32, 1, 2, 16, WIDTH), lambda r: (0, r, 0, 0, 0))
    return pl.pallas_call(
        grid_kernel,
        grid=(rows,),
        in_specs=[block] + [whole(w) for w in weights],
        out_specs=block,
        out_shape=jax.ShapeDtypeStruct(landed.shape, BF16),
        compiler_params=pltpu.CompilerParams(
            dimension_semantics=("arbitrary",), vmem_limit_bytes=VMEM_LIMIT
        ),
        cost_estimate=pl.CostEstimate(
            flops=3_000_000_000, bytes_accessed=2_500_000, transcendentals=1_000_000
        ),
        name="grid_stage",
    )(landed, *weights)


def shift(values, axis, step, count):
    pairs = [(i, i + step) for i in range(count) if 0 <= i + step < count]
    return lax.ppermute(values, axis, pairs)


LON = ("j", "m")


def per_device(
    field,
    norm_gain,
    expand_weight,
    expand_bias,
    depth_kernel,
    depth_bias,
    project_weight,
    block_gain,
    block_qkv,
    block_out,
    grid_gain,
    grid_qkv,
    grid_out,
):
    lat_count, lon_count = 4, 32
    north = shift(field[-1:], "lat", 1, lat_count)
    south = shift(field[:1], "lat", -1, lat_count)

    def side(at):
        return jnp.concatenate([north[:, at], field[:, at], south[:, at]], axis=0)

    left = shift(side(COLS - 1), LON, 1, lon_count)
    right = shift(side(0), LON, -1, lon_count)

    def bands(column):
        middle = column[1:129].reshape(16, 8, WIDTH).transpose(1, 0, 2)
        first = jnp.concatenate([column[None, :1], middle[7:, :15]], axis=1)
        last = jnp.concatenate([middle[:1, 1:], column[None, 129:]], axis=1)
        return jnp.concatenate([first, middle, last], axis=0)

    sides = jnp.concatenate([bands(left), bands(right)], axis=1)
    local_weights = (
        norm_gain[None],
        expand_weight,
        expand_bias[None],
        depth_kernel.reshape(9, WIDE),
        depth_bias[None],
        project_weight,
        block_gain[None],
        block_qkv,
        block_out,
    )
    grid_weights = (grid_gain[None], grid_qkv, grid_out)
    shape = (32, 64, WIDTH)
    inner = local_stage((1, 2), field, north, south, None, local_weights)
    sides, inner = lax.optimization_barrier((sides, inner))
    outer = local_stage((0, 3), field, north, south, sides, local_weights)
    landed = [
        lax.all_to_all(parcels.reshape(shape), ("lat", "j"), 0, 0, tiled=True) for parcels in (inner, outer)
    ]
    results = []
    for groups in landed:
        groups = grid_stage(groups.reshape(32, 2, 2, 16, WIDTH), grid_weights)
        back = lax.all_to_all(groups.reshape(shape), ("lat", "j"), 0, 0, tiled=True)
        results.append(back.reshape(64, 2, 16, WIDTH))
    inner, outer = results
    whole = jnp.concatenate([outer[:, :, :8], inner, outer[:, :, 8:]], axis=2)
    return whole.transpose(1, 0, 2, 3).reshape(128, COLS, WIDTH)


def solution(mesh):
    inner = Mesh(mesh.devices.reshape(4, 8, 4), ("lat", "j", "m"))
    return jax.shard_map(
        per_device,
        mesh=inner,
        in_specs=(P("lat", LON, None),) + (P(),) * 12,
        out_specs=P("lat", LON, None),
        check_vma=False,
    )
```

```python
import functools
import math

import jax
import jax.numpy as jnp
from jax import lax
from jax.experimental import pallas as pl
from jax.experimental.pallas import tpu as pltpu
from jax.sharding import Mesh
from jax.sharding import PartitionSpec as P

HEADS = 8
WIDTH = 256
HEAD = WIDTH // HEADS
WIDE = 1024
COLS = 32
SLICE = 256
F32 = jnp.float32
BF16 = jnp.bfloat16
VMEM_LIMIT = 56 * 1024 * 1024


def norm_rows(values, gain):
    mean = jnp.mean(values, axis=-1, keepdims=True)
    centred = values - mean
    var = jnp.mean(centred * centred, axis=-1, keepdims=True)
    return centred * lax.rsqrt(var + 1e-05) * gain


def double_gelu(x):
    c0 = jnp.asarray(0.7978845608028654, x.dtype)
    c1 = jnp.asarray(0.7978845608028654 * 0.044715, x.dtype)
    return x + x * jnp.tanh(x * (c0 + c1 * (x * x)))


def swap_matrix():
    i = lax.broadcasted_iota(jnp.int32, (256, 256), 0)
    j = lax.broadcasted_iota(jnp.int32, (256, 256), 1)
    return jnp.where((i % 16) * 16 + i // 16 == j, 1.0, 0.0).astype(BF16)


def attend(tokens, gain, w_qkv, w_out):
    count = tokens.shape[0]
    normed = norm_rows(tokens, gain).astype(BF16)
    scale = HEAD ** -0.5 * math.log2(math.e)
    w_qv_t = jnp.concatenate([w_qkv[:, :WIDTH], w_qkv[:, 2 * WIDTH :]], axis=1).T
    keys = jnp.dot(normed, w_qkv[:, WIDTH : 2 * WIDTH], preferred_element_type=F32).astype(BF16)
    low = lax.broadcasted_iota(jnp.int32, (HEAD, 128), 1) < 64
    zero = jnp.zeros((64, 128), BF16)
    none = jnp.zeros((HEAD, 128), BF16)
    q_t, v_t = [], []
    for i in range(count // 256):
        qv = lax.dot_general(
            w_qv_t,
            normed[256 * i : 256 * (i + 1)],
            (((1,), (1,)), ((), ())),
            preferred_element_type=F32,
        )
        q_t += [(qv[:WIDTH, 128 * a : 128 * (a + 1)] * scale).astype(BF16) for a in range(2)]
        v_t += [qv[WIDTH:, 128 * a : 128 * (a + 1)].astype(BF16) for a in range(2)]
    scores = {}
    for n, here in enumerate(q_t):
        over = jnp.concatenate([here[:, 64:], here[:, :64]], axis=1)
        for g in range(2):
            straight, crossed = (here, over) if g == 0 else (over, here)
            row0 = 128 * n + 64 * g
            for t in range(2):
                pair = []
                for jj in range(2):
                    at = 128 * t + 64 * jj
                    first = jnp.where(low, straight[at : at + HEAD], none)
                    second = jnp.where(low, none, crossed[at + HEAD : at + 64])
                    pair.append(jnp.concatenate([first, second], axis=0))
                rhs = jnp.concatenate(
                    [
                        jnp.concatenate([pair[0], zero], axis=1),
                        jnp.concatenate([zero, pair[1]], axis=1),
                    ],
                    axis=0,
                )
                scores[n, g, t] = jnp.dot(
                    keys[row0 : row0 + 64, 128 * t : 128 * (t + 1)], rhs, preferred_element_type=F32
                )
    probs, inverse = {}, {}
    for at, score in scores.items():
        weights = jnp.exp2(score - jnp.max(score, axis=0, keepdims=True))
        inverse[at] = 1.0 / jnp.sum(weights, axis=0, keepdims=True)
        probs[at] = weights.astype(BF16)
    raw = {}
    for n in range(count // 128):
        for j in range(4):
            t, jj = j // 2, j % 2
            lanes = slice(128 * jj, 128 * (jj + 1))
            p0, p1 = probs[n, 0, t][:, lanes], probs[n, 1, t][:, lanes]
            rhs = jnp.concatenate(
                [jnp.concatenate([p0, zero], axis=1), jnp.concatenate([zero, p1], axis=1)], axis=0
            )
            raw[n, j] = jnp.dot(v_t[n][64 * j : 64 * (j + 1)], rhs, preferred_element_type=F32)
    mixed = []
    for n in range(count // 128):
        outs = []
        for j in range(4):
            t, jj = j // 2, j % 2
            lanes = slice(128 * jj, 128 * (jj + 1))
            o0 = raw[n, j][:, :128] * inverse[n, 0, t][:, lanes]
            o1 = raw[n, j][:, 128:] * inverse[n, 1, t][:, lanes]
            outs.append(jnp.where(low, o0[:HEAD], pltpu.roll(o1[:HEAD], 64, 1)).astype(BF16))
            outs.append(jnp.where(low, pltpu.roll(o0[HEAD:], 64, 1), o1[HEAD:]).astype(BF16))
        mixed.append(jnp.concatenate(outs, axis=0).T)
    mixed = jnp.concatenate(mixed, axis=0)
    return tokens + jnp.dot(mixed, w_out, preferred_element_type=F32)


def local_kernel(
    blocks,
    field_ref,
    north_ref,
    south_ref,
    *refs,
):
    edge = 0 in blocks
    if edge:
        side_ref, refs = refs[0], refs[1:]
    (
        gain_ref,
        w_expand_ref,
        b_expand_ref,
        depth_ref,
        b_depth_ref,
        w_project_ref,
        gain2_ref,
        w_qkv_ref,
        w_out_ref,
        out_ref,
        normed_ref,
        grown_ref,
        filtered_ref,
        acc_ref,
    ) = refs
    row = lax.broadcasted_iota(jnp.int32, (160, 512), 0)
    lane = lax.broadcasted_iota(jnp.int32, (160, 512), 1)
    same_band = row % 16 == lane // COLS
    col_gap = lane % COLS - row // 16
    k_of = lax.broadcasted_iota(jnp.int32, (160, SLICE), 0) % 16
    lat = lax.axis_index("lat")
    lon = lax.axis_index("j") * lax.axis_size("m") + lax.axis_index("m")
    keep_left = jnp.where(lon == 0, 0.0, 1.0)
    keep_right = jnp.where(lon == 8 * lax.axis_size("m") - 1, 0.0, 1.0)
    keep_top = jnp.where((k_of == 0) & (lat == 0), 0.0, 1.0).astype(BF16)
    keep_bottom = jnp.where((k_of == 15) & (lat == 3), 0.0, 1.0).astype(BF16)
    swap = swap_matrix()
    halves = []
    for block in blocks:
        window = 8 * block - 1
        pick = jnp.where(same_band & (col_gap == window), 1.0, 0.0).astype(BF16)
        on_side = block == 0 or block == COLS // 8 - 1
        if on_side:
            srow = lax.broadcasted_iota(jnp.int32, (160, 32), 0)
            slane = lax.broadcasted_iota(jnp.int32, (160, 32), 1)
            column = 0 if block == 0 else 9
            lane0 = 0 if block == 0 else 16
            pick_side = jnp.where(
                (srow // 16 == column) & (srow % 16 + lane0 == slane), 1.0, 0.0
            ).astype(BF16)
        for r in range(10):
            if r == 0:
                rows = jnp.concatenate(
                    [north_ref[...]] + [field_ref[8 * k + 7 : 8 * k + 8] for k in range(15)], axis=0
                )
            elif r == 9:
                rows = jnp.concatenate(
                    [field_ref[8 * k : 8 * k + 1] for k in range(1, 16)] + [south_ref[...]], axis=0
                )
            else:
                rows = jnp.concatenate(
                    [field_ref[8 * k + r - 1 : 8 * k + r] for k in range(16)], axis=0
                )
            cells = jnp.dot(pick, rows.reshape(512, WIDTH), preferred_element_type=F32)
            if on_side:
                cells = cells + jnp.dot(pick_side, side_ref[r], preferred_element_type=F32)
            if 1 <= r <= 8:
                acc_ref[128 * (r - 1) : 128 * r] = cells[16:144]
            normed_ref[160 * r : 160 * (r + 1)] = norm_rows(cells, gain_ref[...]).astype(BF16)

        def channels(s):
            at = pl.ds(pl.multiple_of(s * SLICE, SLICE), SLICE)
            bias = jnp.broadcast_to(b_expand_ref[:, at], (16, SLICE)).astype(BF16)
            bias = jnp.concatenate([bias] * 10, axis=0)
            w_here = w_expand_ref[:, at]
            grown = jnp.dot(normed_ref[...], w_here, preferred_element_type=F32).astype(BF16)
            for r in range(10):
                g = double_gelu(grown[160 * r : 160 * (r + 1)] + bias)
                if r == 0:
                    g = g * keep_top
                if r == 9:
                    g = g * keep_bottom
                if on_side:
                    keep = keep_left if block == 0 else keep_right
                    if block == 0:
                        g = jnp.concatenate([(g[:16] * keep.astype(BF16)), g[16:]], axis=0)
                    else:
                        g = jnp.concatenate([g[:144], (g[144:] * keep.astype(BF16))], axis=0)
                grown_ref[r] = g.reshape(10, 16, SLICE)
            for half in range(SLICE // 128):
                lanes = slice(128 * half, 128 * (half + 1))
                there = pl.ds(pl.multiple_of(s * SLICE + 128 * half, 128), 128)
                taps = [
                    jnp.broadcast_to(0.5 * depth_ref[i // 3, i % 3 : i % 3 + 1, there], (16, 128)).astype(BF16)
                    for i in range(9)
                ]
                depth_bias = jnp.broadcast_to(b_depth_ref[:, there], (16, 128)).astype(BF16)
                for c in range(8):
                    near = [[grown_ref[r, c + dj, :, lanes] for r in range(10)] for dj in range(3)]
                    for r in range(8):
                        p = [
                            taps[dj] * near[dj][r]
                            + taps[3 + dj] * near[dj][r + 1]
                            + taps[6 + dj] * near[dj][r + 2]
                            for dj in range(3)
                        ]
                        total = (p[0] + p[1]) + (p[2] + depth_bias)
                        filtered_ref[r, c, :, lanes] = double_gelu(total)
            acc_ref[...] += jnp.dot(
                filtered_ref[...].reshape(1024, SLICE),
                w_project_ref[at, :] * jnp.asarray(0.5, BF16),
                preferred_element_type=F32,
            )

        lax.fori_loop(0, WIDE // SLICE, lambda s, c: (channels(s), c)[1], 0)
        mixed = acc_ref[...].astype(BF16)
        turned = [
            jnp.dot(swap, mixed[256 * i : 256 * (i + 1)], preferred_element_type=F32) for i in range(4)
        ]
        tokens = jnp.concatenate(
            [turned[i][16 * k : 16 * k + 16] for k in range(16) for i in range(4)], axis=0
        )
        halves.append(attend(tokens, gain2_ref[...], w_qkv_ref[...], w_out_ref[...]))
    for k in range(16):
        both = jnp.concatenate(
            [halves[h][64 * k : 64 * k + 64].reshape(8, 8, WIDTH) for h in range(2)], axis=1
        )
        out_ref[8 * (k % 8) : 8 * (k % 8) + 8, k // 8] = both.astype(BF16)


def local_stage(blocks, field, north, south, side, weights):
    vmem = pl.BlockSpec(memory_space=pltpu.VMEM)
    arrays = (field, north, south) + ((side,) if 0 in blocks else ()) + weights
    return pl.pallas_call(
        functools.partial(local_kernel, blocks),
        in_specs=[vmem] * len(arrays),
        out_specs=vmem,
        out_shape=jax.ShapeDtypeStruct((64, 2, 16, WIDTH), BF16),
        scratch_shapes=[
            pltpu.VMEM((1600, WIDTH), BF16),
            pltpu.VMEM((10, 10, 16, SLICE), BF16),
            pltpu.VMEM((8, 8, 16, SLICE), BF16),
            pltpu.VMEM((1024, WIDTH), F32),
        ],
        compiler_params=pltpu.CompilerParams(vmem_limit_bytes=VMEM_LIMIT),
        cost_estimate=pl.CostEstimate(
            flops=5_000_000_000, bytes_accessed=3_000_000, transcendentals=6_000_000
        ),
        name="local_stage",
    )(*arrays)


def grid_kernel(in_ref, gain_ref, w_qkv_ref, w_out_ref, *refs):
    out_ref = refs[-1]
    swap = swap_matrix()
    turned = []
    for c in range(4):
        block = in_ref[8 * c : 8 * c + 8].reshape(256, WIDTH)
        turned.append(jnp.dot(swap, block, preferred_element_type=F32))
    tokens = jnp.concatenate(
        [turned[c][16 * k : 16 * k + 16] for k in range(16) for c in range(4)], axis=0
    )
    done = attend(tokens, gain_ref[...], w_qkv_ref[...], w_out_ref[...]).astype(BF16)
    for c in range(4):
        block = jnp.concatenate([done[64 * k + 16 * c : 64 * k + 16 * c + 16] for k in range(16)], axis=0)
        back = jnp.dot(swap, block, preferred_element_type=F32).astype(BF16)
        out_ref[8 * c : 8 * c + 8] = back.reshape(8, 1, 1, 2, 16, WIDTH)


def grid_stage(part, landed, weights, done):
    whole = lambda a: pl.BlockSpec(a.shape, lambda r: (0,) * a.ndim)
    block = pl.BlockSpec((32, 1, 2, 16, WIDTH), lambda r: (0, r, 0, 0, 0))
    more = () if done is None else (done,)
    return pl.pallas_call(
        grid_kernel,
        grid=(2,),
        in_specs=[block]
        + [whole(w) for w in weights]
        + [pl.BlockSpec(memory_space=pl.ANY)] * len(more),
        out_specs=pl.BlockSpec((32, 1, 1, 2, 16, WIDTH), lambda r: (0, part, r, 0, 0, 0)),
        out_shape=jax.ShapeDtypeStruct((32, 2, 2, 2, 16, WIDTH), BF16),
        input_output_aliases={4: 0} if more else {},
        compiler_params=pltpu.CompilerParams(
            dimension_semantics=("arbitrary",), vmem_limit_bytes=VMEM_LIMIT
        ),
        cost_estimate=pl.CostEstimate(
            flops=3_000_000_000, bytes_accessed=2_500_000, transcendentals=1_000_000
        ),
        name="grid_stage",
    )(landed, *weights, *more)


def shift(values, axis, step, count):
    pairs = [(i, i + step) for i in range(count) if 0 <= i + step < count]
    return lax.ppermute(values, axis, pairs)


LON = ("j", "m")


def per_device(
    field,
    norm_gain,
    expand_weight,
    expand_bias,
    depth_kernel,
    depth_bias,
    project_weight,
    block_gain,
    block_qkv,
    block_out,
    grid_gain,
    grid_qkv,
    grid_out,
):
    lat_count, lon_count = 4, 32
    north = shift(field[-1:], "lat", 1, lat_count)
    south = shift(field[:1], "lat", -1, lat_count)

    def side(at):
        return jnp.concatenate([north[:, at], field[:, at], south[:, at]], axis=0)

    left = shift(side(COLS - 1), LON, 1, lon_count)
    right = shift(side(0), LON, -1, lon_count)

    def bands(column):
        middle = column[1:129].reshape(16, 8, WIDTH).transpose(1, 0, 2)
        first = jnp.concatenate([column[None, :1], middle[7:, :15]], axis=1)
        last = jnp.concatenate([middle[:1, 1:], column[None, 129:]], axis=1)
        return jnp.concatenate([first, middle, last], axis=0)

    sides = jnp.concatenate([bands(left), bands(right)], axis=1)
    local_weights = (
        norm_gain[None],
        expand_weight,
        expand_bias[None],
        depth_kernel,
        depth_bias[None],
        project_weight,
        block_gain[None],
        block_qkv,
        block_out,
    )
    grid_weights = (grid_gain[None], grid_qkv, grid_out)
    shape = (32, 64, WIDTH)
    exchange = lambda parcels: lax.all_to_all(parcels.reshape(shape), ("lat", "j"), 0, 0, tiled=True)
    inner = local_stage((1, 2), field, north, south, None, local_weights)
    inner_landed = exchange(inner)
    sides, _ = lax.optimization_barrier((sides, inner))
    outer = local_stage((0, 3), field, north, south, sides, local_weights)
    outer, _ = lax.optimization_barrier((outer, inner_landed))
    outer_landed = exchange(outer)
    pieces = (32, 2, 2, 16, WIDTH)
    done = grid_stage(0, inner_landed.reshape(pieces), grid_weights, None)
    done = grid_stage(1, outer_landed.reshape(pieces), grid_weights, done)
    back = lax.all_to_all(done.reshape(32, 128, WIDTH), ("lat", "j"), 0, 0, tiled=True)
    back = back.reshape(32, 2, 2, 2, 16, WIDTH)
    inner, outer = (back[:, part].reshape(64, 2, 16, WIDTH) for part in range(2))
    whole = jnp.concatenate([outer[:, :, :8], inner, outer[:, :, 8:]], axis=2)
    return whole.transpose(1, 0, 2, 3).reshape(128, COLS, WIDTH)


def solution(mesh):
    inner = Mesh(mesh.devices.reshape(4, 8, 4), ("lat", "j", "m"))
    return jax.shard_map(
        per_device,
        mesh=inner,
        in_specs=(P("lat", LON, None),) + (P(),) * 12,
        out_specs=P("lat", LON, None),
        check_vma=False,
    )
```

```python
import functools
import math

import jax
import jax.numpy as jnp
from jax import lax
from jax.experimental import pallas as pl
from jax.experimental.pallas import tpu as pltpu
from jax.sharding import Mesh
from jax.sharding import PartitionSpec as P

HEADS = 8
WIDTH = 256
HEAD = WIDTH // HEADS
WIDE = 1024
COLS = 32
SLICE = 256
F32 = jnp.float32
BF16 = jnp.bfloat16
VMEM_LIMIT = 56 * 1024 * 1024


def norm_rows(values, gain):
    mean = jnp.mean(values, axis=-1, keepdims=True)
    centred = values - mean
    var = jnp.mean(centred * centred, axis=-1, keepdims=True)
    return centred * lax.rsqrt(var + 1e-05) * gain


def double_gelu(x):
    c0 = jnp.asarray(0.7978845608028654, x.dtype)
    c1 = jnp.asarray(0.7978845608028654 * 0.044715, x.dtype)
    return x + x * jnp.tanh(x * (c0 + c1 * (x * x)))


def swap_matrix():
    i = lax.broadcasted_iota(jnp.int32, (256, 256), 0)
    j = lax.broadcasted_iota(jnp.int32, (256, 256), 1)
    return jnp.where((i % 16) * 16 + i // 16 == j, 1.0, 0.0).astype(BF16)


def attend(tokens, gain, w_qkv, w_out):
    count = tokens.shape[0]
    normed = norm_rows(tokens, gain).astype(BF16)
    scale = HEAD ** -0.5 * math.log2(math.e)
    w_qv_t = jnp.concatenate([w_qkv[:, :WIDTH], w_qkv[:, 2 * WIDTH :]], axis=1).T
    keys = jnp.dot(normed, w_qkv[:, WIDTH : 2 * WIDTH], preferred_element_type=F32).astype(BF16)
    low = lax.broadcasted_iota(jnp.int32, (HEAD, 128), 1) < 64
    zero = jnp.zeros((64, 128), BF16)
    none = jnp.zeros((HEAD, 128), BF16)
    q_t, v_t = [], []
    for i in range(count // 256):
        qv = lax.dot_general(
            w_qv_t,
            normed[256 * i : 256 * (i + 1)],
            (((1,), (1,)), ((), ())),
            preferred_element_type=F32,
        )
        q_t += [(qv[:WIDTH, 128 * a : 128 * (a + 1)] * scale).astype(BF16) for a in range(2)]
        v_t += [qv[WIDTH:, 128 * a : 128 * (a + 1)].astype(BF16) for a in range(2)]
    scores = {}
    for n, here in enumerate(q_t):
        over = jnp.concatenate([here[:, 64:], here[:, :64]], axis=1)
        for g in range(2):
            straight, crossed = (here, over) if g == 0 else (over, here)
            row0 = 128 * n + 64 * g
            for t in range(2):
                pair = []
                for jj in range(2):
                    at = 128 * t + 64 * jj
                    first = jnp.where(low, straight[at : at + HEAD], none)
                    second = jnp.where(low, none, crossed[at + HEAD : at + 64])
                    pair.append(jnp.concatenate([first, second], axis=0))
                rhs = jnp.concatenate(
                    [
                        jnp.concatenate([pair[0], zero], axis=1),
                        jnp.concatenate([zero, pair[1]], axis=1),
                    ],
                    axis=0,
                )
                scores[n, g, t] = jnp.dot(
                    keys[row0 : row0 + 64, 128 * t : 128 * (t + 1)], rhs, preferred_element_type=F32
                )
    probs, inverse = {}, {}
    for at, score in scores.items():
        weights = jnp.exp2(score - jnp.max(score, axis=0, keepdims=True))
        inverse[at] = 1.0 / jnp.sum(weights, axis=0, keepdims=True)
        probs[at] = weights.astype(BF16)
    raw = {}
    for n in range(count // 128):
        for j in range(4):
            t, jj = j // 2, j % 2
            lanes = slice(128 * jj, 128 * (jj + 1))
            p0, p1 = probs[n, 0, t][:, lanes], probs[n, 1, t][:, lanes]
            rhs = jnp.concatenate(
                [jnp.concatenate([p0, zero], axis=1), jnp.concatenate([zero, p1], axis=1)], axis=0
            )
            raw[n, j] = jnp.dot(v_t[n][64 * j : 64 * (j + 1)], rhs, preferred_element_type=F32)
    mixed = []
    for n in range(count // 128):
        outs = []
        for j in range(4):
            t, jj = j // 2, j % 2
            lanes = slice(128 * jj, 128 * (jj + 1))
            o0 = raw[n, j][:, :128] * inverse[n, 0, t][:, lanes]
            o1 = raw[n, j][:, 128:] * inverse[n, 1, t][:, lanes]
            outs.append(jnp.where(low, o0[:HEAD], pltpu.roll(o1[:HEAD], 64, 1)).astype(BF16))
            outs.append(jnp.where(low, pltpu.roll(o0[HEAD:], 64, 1), o1[HEAD:]).astype(BF16))
        mixed.append(jnp.concatenate(outs, axis=0).T)
    mixed = jnp.concatenate(mixed, axis=0)
    return tokens + jnp.dot(mixed, w_out, preferred_element_type=F32)


def local_kernel(
    blocks,
    field_ref,
    north_ref,
    south_ref,
    *refs,
):
    edge = 0 in blocks
    if edge:
        side_ref, refs = refs[0], refs[1:]
    (
        gain_ref,
        w_expand_ref,
        b_expand_ref,
        depth_ref,
        b_depth_ref,
        w_project_ref,
        gain2_ref,
        w_qkv_ref,
        w_out_ref,
        out_ref,
        normed_ref,
        grown_ref,
        filtered_ref,
        acc_ref,
    ) = refs
    row = lax.broadcasted_iota(jnp.int32, (160, 512), 0)
    lane = lax.broadcasted_iota(jnp.int32, (160, 512), 1)
    same_band = row % 16 == lane // COLS
    col_gap = lane % COLS - row // 16
    k_of = lax.broadcasted_iota(jnp.int32, (160, SLICE), 0) % 16
    lat = lax.axis_index("lat")
    lon = lax.axis_index("j") * lax.axis_size("m") + lax.axis_index("m")
    keep_left = jnp.where(lon == 0, 0.0, 1.0)
    keep_right = jnp.where(lon == 8 * lax.axis_size("m") - 1, 0.0, 1.0)
    keep_top = jnp.where((k_of == 0) & (lat == 0), 0.0, 1.0).astype(BF16)
    keep_bottom = jnp.where((k_of == 15) & (lat == 3), 0.0, 1.0).astype(BF16)
    swap = swap_matrix()
    halves = []
    for block in blocks:
        window = 8 * block - 1
        pick = jnp.where(same_band & (col_gap == window), 1.0, 0.0).astype(BF16)
        on_side = block == 0 or block == COLS // 8 - 1
        if on_side:
            srow = lax.broadcasted_iota(jnp.int32, (160, 32), 0)
            slane = lax.broadcasted_iota(jnp.int32, (160, 32), 1)
            column = 0 if block == 0 else 9
            lane0 = 0 if block == 0 else 16
            pick_side = jnp.where(
                (srow // 16 == column) & (srow % 16 + lane0 == slane), 1.0, 0.0
            ).astype(BF16)
        for r in range(10):
            if r == 0:
                rows = jnp.concatenate(
                    [north_ref[...]] + [field_ref[8 * k + 7 : 8 * k + 8] for k in range(15)], axis=0
                )
            elif r == 9:
                rows = jnp.concatenate(
                    [field_ref[8 * k : 8 * k + 1] for k in range(1, 16)] + [south_ref[...]], axis=0
                )
            else:
                rows = jnp.concatenate(
                    [field_ref[8 * k + r - 1 : 8 * k + r] for k in range(16)], axis=0
                )
            cells = jnp.dot(pick, rows.reshape(512, WIDTH), preferred_element_type=F32)
            if on_side:
                cells = cells + jnp.dot(pick_side, side_ref[r], preferred_element_type=F32)
            if 1 <= r <= 8:
                acc_ref[128 * (r - 1) : 128 * r] = cells[16:144]
            normed_ref[160 * r : 160 * (r + 1)] = norm_rows(cells, gain_ref[...]).astype(BF16)

        def channels(s):
            at = pl.ds(pl.multiple_of(s * SLICE, SLICE), SLICE)
            bias = jnp.broadcast_to(b_expand_ref[:, at], (16, SLICE)).astype(BF16)
            bias = jnp.concatenate([bias] * 10, axis=0)
            w_here = w_expand_ref[:, at]
            grown = jnp.dot(normed_ref[...], w_here, preferred_element_type=F32).astype(BF16)
            for r in range(10):
                g = double_gelu(grown[160 * r : 160 * (r + 1)] + bias)
                if r == 0:
                    g = g * keep_top
                if r == 9:
                    g = g * keep_bottom
                if on_side:
                    keep = keep_left if block == 0 else keep_right
                    if block == 0:
                        g = jnp.concatenate([(g[:16] * keep.astype(BF16)), g[16:]], axis=0)
                    else:
                        g = jnp.concatenate([g[:144], (g[144:] * keep.astype(BF16))], axis=0)
                grown_ref[r] = g.reshape(10, 16, SLICE)
            for half in range(SLICE // 128):
                lanes = slice(128 * half, 128 * (half + 1))
                there = pl.ds(pl.multiple_of(s * SLICE + 128 * half, 128), 128)
                taps = [
                    jnp.broadcast_to(0.5 * depth_ref[i // 3, i % 3 : i % 3 + 1, there], (16, 128)).astype(BF16)
                    for i in range(9)
                ]
                depth_bias = jnp.broadcast_to(b_depth_ref[:, there], (16, 128)).astype(BF16)
                for c in range(8):
                    near = [[grown_ref[r, c + dj, :, lanes] for r in range(10)] for dj in range(3)]
                    for r in range(8):
                        p = [
                            taps[dj] * near[dj][r]
                            + taps[3 + dj] * near[dj][r + 1]
                            + taps[6 + dj] * near[dj][r + 2]
                            for dj in range(3)
                        ]
                        total = (p[0] + p[1]) + (p[2] + depth_bias)
                        filtered_ref[r, c, :, lanes] = double_gelu(total)
            acc_ref[...] += jnp.dot(
                filtered_ref[...].reshape(1024, SLICE),
                w_project_ref[at, :] * jnp.asarray(0.5, BF16),
                preferred_element_type=F32,
            )

        def two_slices(s, carry):
            channels(2 * s)
            channels(2 * s + 1)
            return carry

        lax.fori_loop(0, WIDE // SLICE // 2, two_slices, 0)
        mixed = acc_ref[...].astype(BF16)
        turned = [
            jnp.dot(swap, mixed[256 * i : 256 * (i + 1)], preferred_element_type=F32) for i in range(4)
        ]
        tokens = jnp.concatenate(
            [turned[i][16 * k : 16 * k + 16] for k in range(16) for i in range(4)], axis=0
        )
        halves.append(attend(tokens, gain2_ref[...], w_qkv_ref[...], w_out_ref[...]))
    for k in range(16):
        both = jnp.concatenate(
            [halves[h][64 * k : 64 * k + 64].reshape(8, 8, WIDTH) for h in range(2)], axis=1
        )
        out_ref[8 * (k % 8) : 8 * (k % 8) + 8, k // 8] = both.astype(BF16)


def local_stage(blocks, field, north, south, side, weights):
    vmem = pl.BlockSpec(memory_space=pltpu.VMEM)
    arrays = (field, north, south) + ((side,) if 0 in blocks else ()) + weights
    return pl.pallas_call(
        functools.partial(local_kernel, blocks),
        in_specs=[vmem] * len(arrays),
        out_specs=vmem,
        out_shape=jax.ShapeDtypeStruct((64, 2, 16, WIDTH), BF16),
        scratch_shapes=[
            pltpu.VMEM((1600, WIDTH), BF16),
            pltpu.VMEM((10, 10, 16, SLICE), BF16),
            pltpu.VMEM((8, 8, 16, SLICE), BF16),
            pltpu.VMEM((1024, WIDTH), F32),
        ],
        compiler_params=pltpu.CompilerParams(vmem_limit_bytes=VMEM_LIMIT),
        cost_estimate=pl.CostEstimate(
            flops=5_000_000_000, bytes_accessed=3_000_000, transcendentals=6_000_000
        ),
        name="local_stage",
    )(*arrays)


def grid_kernel(in_ref, gain_ref, w_qkv_ref, w_out_ref, *refs):
    out_ref = refs[-1]
    swap = swap_matrix()
    turned = []
    for c in range(4):
        block = in_ref[8 * c : 8 * c + 8].reshape(256, WIDTH)
        turned.append(jnp.dot(swap, block, preferred_element_type=F32))
    tokens = jnp.concatenate(
        [turned[c][16 * k : 16 * k + 16] for k in range(16) for c in range(4)], axis=0
    )
    done = attend(tokens, gain_ref[...], w_qkv_ref[...], w_out_ref[...]).astype(BF16)
    for c in range(4):
        block = jnp.concatenate([done[64 * k + 16 * c : 64 * k + 16 * c + 16] for k in range(16)], axis=0)
        back = jnp.dot(swap, block, preferred_element_type=F32)
        at = slice(8 * c, 8 * c + 8)
        if len(refs) == 1:
            out_ref[at] = back.astype(BF16).reshape(8, 1, 2, 16, WIDTH)
        else:
            back = back.reshape(16, 16, WIDTH)
            inner = refs[0][at].astype(F32).reshape(16, 16, WIDTH)
            rows = jnp.concatenate([back[:, :8], inner, back[:, 8:]], axis=1)
            out_ref[at] = rows.astype(BF16).reshape(8, 1, 2, COLS, WIDTH)


def grid_stage(landed, weights, inner):
    whole = lambda a: pl.BlockSpec(a.shape, lambda r: (0,) * a.ndim)
    block = lambda n: pl.BlockSpec((32, 1, 2, n, WIDTH), lambda r: (0, r, 0, 0, 0))
    more = () if inner is None else (inner,)
    columns = COLS if more else 16
    return pl.pallas_call(
        grid_kernel,
        grid=(2,),
        in_specs=[block(16)] + [whole(w) for w in weights] + [block(16)] * len(more),
        out_specs=block(columns),
        out_shape=jax.ShapeDtypeStruct((32, 2, 2, columns, WIDTH), BF16),
        compiler_params=pltpu.CompilerParams(
            dimension_semantics=("arbitrary",), vmem_limit_bytes=VMEM_LIMIT
        ),
        cost_estimate=pl.CostEstimate(
            flops=3_000_000_000, bytes_accessed=2_500_000, transcendentals=1_000_000
        ),
        name="grid_stage",
    )(landed, *weights, *more)


def shift(values, axis, step, count):
    pairs = [(i, i + step) for i in range(count) if 0 <= i + step < count]
    return lax.ppermute(values, axis, pairs)


LON = ("j", "m")


def per_device(
    field,
    norm_gain,
    expand_weight,
    expand_bias,
    depth_kernel,
    depth_bias,
    project_weight,
    block_gain,
    block_qkv,
    block_out,
    grid_gain,
    grid_qkv,
    grid_out,
):
    lat_count, lon_count = 4, 32
    north = shift(field[-1:], "lat", 1, lat_count)
    south = shift(field[:1], "lat", -1, lat_count)

    def side(at):
        return jnp.concatenate([north[:, at], field[:, at], south[:, at]], axis=0)

    left = shift(side(COLS - 1), LON, 1, lon_count)
    right = shift(side(0), LON, -1, lon_count)

    def bands(column):
        middle = column[1:129].reshape(16, 8, WIDTH).transpose(1, 0, 2)
        first = jnp.concatenate([column[None, :1], middle[7:, :15]], axis=1)
        last = jnp.concatenate([middle[:1, 1:], column[None, 129:]], axis=1)
        return jnp.concatenate([first, middle, last], axis=0)

    sides = jnp.concatenate([bands(left), bands(right)], axis=1)
    local_weights = (
        norm_gain[None],
        expand_weight,
        expand_bias[None],
        depth_kernel,
        depth_bias[None],
        project_weight,
        block_gain[None],
        block_qkv,
        block_out,
    )
    grid_weights = (grid_gain[None], grid_qkv, grid_out)
    shape = (32, 64, WIDTH)
    exchange = lambda parcels: lax.all_to_all(parcels.reshape(shape), ("lat", "j"), 0, 0, tiled=True)
    inner = local_stage((1, 2), field, north, south, None, local_weights)
    inner_landed = exchange(inner)
    sides, _ = lax.optimization_barrier((sides, inner))
    outer = local_stage((0, 3), field, north, south, sides, local_weights)
    outer, _ = lax.optimization_barrier((outer, inner_landed))
    outer_landed = exchange(outer)
    pieces = (32, 2, 2, 16, WIDTH)
    done = grid_stage(inner_landed.reshape(pieces), grid_weights, None)
    done = grid_stage(outer_landed.reshape(pieces), grid_weights, done)
    back = lax.all_to_all(done.reshape(32, 128, WIDTH), ("lat", "j"), 0, 0, tiled=True)
    return back.reshape(64, 2, COLS, WIDTH).transpose(1, 0, 2, 3).reshape(128, COLS, WIDTH)


def solution(mesh):
    inner = Mesh(mesh.devices.reshape(4, 8, 4), ("lat", "j", "m"))
    return jax.shard_map(
        per_device,
        mesh=inner,
        in_specs=(P("lat", LON, None),) + (P(),) * 12,
        out_specs=P("lat", LON, None),
        check_vma=False,
    )
```

```python
import functools
import math

import jax
import jax.numpy as jnp
from jax import lax
from jax.experimental import pallas as pl
from jax.experimental.pallas import tpu as pltpu
from jax.sharding import Mesh
from jax.sharding import PartitionSpec as P

HEADS = 8
WIDTH = 256
HEAD = WIDTH // HEADS
WIDE = 1024
COLS = 32
SLICE = 256
F32 = jnp.float32
BF16 = jnp.bfloat16
VMEM_LIMIT = 56 * 1024 * 1024


def norm_rows(values, gain):
    mean = jnp.mean(values, axis=-1, keepdims=True)
    centred = values - mean
    var = jnp.mean(centred * centred, axis=-1, keepdims=True)
    return centred * lax.rsqrt(var + 1e-05) * gain


def double_gelu(x):
    c0 = jnp.asarray(0.7978845608028654, x.dtype)
    c1 = jnp.asarray(0.7978845608028654 * 0.044715, x.dtype)
    return x + x * jnp.tanh(x * (c0 + c1 * (x * x)))


def swap_matrix():
    i = lax.broadcasted_iota(jnp.int32, (256, 256), 0)
    j = lax.broadcasted_iota(jnp.int32, (256, 256), 1)
    return jnp.where((i % 16) * 16 + i // 16 == j, 1.0, 0.0).astype(BF16)


def attend(tokens, gain, w_qkv, w_out):
    count = tokens.shape[0]
    normed = norm_rows(tokens, gain).astype(BF16)
    scale = HEAD ** -0.5 * math.log2(math.e)
    w_qv_t = jnp.concatenate([w_qkv[:, :WIDTH], w_qkv[:, 2 * WIDTH :]], axis=1).T
    keys = jnp.dot(normed, w_qkv[:, WIDTH : 2 * WIDTH], preferred_element_type=F32).astype(BF16)
    low = lax.broadcasted_iota(jnp.int32, (HEAD, 128), 1) < 64
    zero = jnp.zeros((64, 128), BF16)
    none = jnp.zeros((HEAD, 128), BF16)
    q_t, v_t = [], []
    for i in range(count // 256):
        qv = lax.dot_general(
            w_qv_t,
            normed[256 * i : 256 * (i + 1)],
            (((1,), (1,)), ((), ())),
            preferred_element_type=F32,
        )
        q_t += [(qv[:WIDTH, 128 * a : 128 * (a + 1)] * scale).astype(BF16) for a in range(2)]
        v_t += [qv[WIDTH:, 128 * a : 128 * (a + 1)].astype(BF16) for a in range(2)]
    scores = {}
    for n, here in enumerate(q_t):
        over = jnp.concatenate([here[:, 64:], here[:, :64]], axis=1)
        for g in range(2):
            straight, crossed = (here, over) if g == 0 else (over, here)
            row0 = 128 * n + 64 * g
            for t in range(2):
                pair = []
                for jj in range(2):
                    at = 128 * t + 64 * jj
                    first = jnp.where(low, straight[at : at + HEAD], none)
                    second = jnp.where(low, none, crossed[at + HEAD : at + 64])
                    pair.append(jnp.concatenate([first, second], axis=0))
                rhs = jnp.concatenate(
                    [
                        jnp.concatenate([pair[0], zero], axis=1),
                        jnp.concatenate([zero, pair[1]], axis=1),
                    ],
                    axis=0,
                )
                scores[n, g, t] = jnp.dot(
                    keys[row0 : row0 + 64, 128 * t : 128 * (t + 1)], rhs, preferred_element_type=F32
                )
    probs, inverse = {}, {}
    for at, score in scores.items():
        weights = jnp.exp2(score - jnp.max(score, axis=0, keepdims=True))
        inverse[at] = 1.0 / jnp.sum(weights, axis=0, keepdims=True)
        probs[at] = weights.astype(BF16)
    raw = {}
    for n in range(count // 128):
        for j in range(4):
            t, jj = j // 2, j % 2
            lanes = slice(128 * jj, 128 * (jj + 1))
            p0, p1 = probs[n, 0, t][:, lanes], probs[n, 1, t][:, lanes]
            rhs = jnp.concatenate(
                [jnp.concatenate([p0, zero], axis=1), jnp.concatenate([zero, p1], axis=1)], axis=0
            )
            raw[n, j] = jnp.dot(v_t[n][64 * j : 64 * (j + 1)], rhs, preferred_element_type=F32)
    mixed = []
    for n in range(count // 128):
        outs = []
        for j in range(4):
            t, jj = j // 2, j % 2
            lanes = slice(128 * jj, 128 * (jj + 1))
            o0 = raw[n, j][:, :128] * inverse[n, 0, t][:, lanes]
            o1 = raw[n, j][:, 128:] * inverse[n, 1, t][:, lanes]
            outs.append(jnp.where(low, o0[:HEAD], pltpu.roll(o1[:HEAD], 64, 1)).astype(BF16))
            outs.append(jnp.where(low, pltpu.roll(o0[HEAD:], 64, 1), o1[HEAD:]).astype(BF16))
        mixed.append(jnp.concatenate(outs, axis=0).T)
    mixed = jnp.concatenate(mixed, axis=0)
    return tokens + jnp.dot(mixed, w_out, preferred_element_type=F32)


def local_kernel(
    blocks,
    field_ref,
    north_ref,
    south_ref,
    *refs,
):
    edge = 0 in blocks
    if edge:
        side_ref, refs = refs[0], refs[1:]
    (
        gain_ref,
        w_expand_ref,
        b_expand_ref,
        depth_ref,
        b_depth_ref,
        w_project_ref,
        gain2_ref,
        w_qkv_ref,
        w_out_ref,
        out_ref,
        normed_ref,
        grown_ref,
        filtered_ref,
        acc_ref,
    ) = refs
    row = lax.broadcasted_iota(jnp.int32, (160, 512), 0)
    lane = lax.broadcasted_iota(jnp.int32, (160, 512), 1)
    same_band = row % 16 == lane // COLS
    col_gap = lane % COLS - row // 16
    k_of = lax.broadcasted_iota(jnp.int32, (160, SLICE), 0) % 16
    lat = lax.axis_index("lat")
    lon = lax.axis_index("j") * lax.axis_size("m") + lax.axis_index("m")
    keep_left = jnp.where(lon == 0, 0.0, 1.0)
    keep_right = jnp.where(lon == 8 * lax.axis_size("m") - 1, 0.0, 1.0)
    keep_top = jnp.where((k_of == 0) & (lat == 0), 0.0, 1.0).astype(BF16)
    keep_bottom = jnp.where((k_of == 15) & (lat == 3), 0.0, 1.0).astype(BF16)
    swap = swap_matrix()
    halves = []
    for block in blocks:
        window = 8 * block - 1
        pick = jnp.where(same_band & (col_gap == window), 1.0, 0.0).astype(BF16)
        on_side = block == 0 or block == COLS // 8 - 1
        if on_side:
            srow = lax.broadcasted_iota(jnp.int32, (160, 32), 0)
            slane = lax.broadcasted_iota(jnp.int32, (160, 32), 1)
            column = 0 if block == 0 else 9
            lane0 = 0 if block == 0 else 16
            pick_side = jnp.where(
                (srow // 16 == column) & (srow % 16 + lane0 == slane), 1.0, 0.0
            ).astype(BF16)
        for r in range(10):
            if r == 0:
                rows = jnp.concatenate(
                    [north_ref[...]] + [field_ref[8 * k + 7 : 8 * k + 8] for k in range(15)], axis=0
                )
            elif r == 9:
                rows = jnp.concatenate(
                    [field_ref[8 * k : 8 * k + 1] for k in range(1, 16)] + [south_ref[...]], axis=0
                )
            else:
                rows = jnp.concatenate(
                    [field_ref[8 * k + r - 1 : 8 * k + r] for k in range(16)], axis=0
                )
            cells = jnp.dot(pick, rows.reshape(512, WIDTH), preferred_element_type=F32)
            if on_side:
                cells = cells + jnp.dot(pick_side, side_ref[r], preferred_element_type=F32)
            if 1 <= r <= 8:
                acc_ref[128 * (r - 1) : 128 * r] = cells[16:144]
            normed_ref[160 * r : 160 * (r + 1)] = norm_rows(cells, gain_ref[...]).astype(BF16)

        def channels(s):
            at = pl.ds(pl.multiple_of(s * SLICE, SLICE), SLICE)
            bias = jnp.broadcast_to(b_expand_ref[:, at], (16, SLICE)).astype(BF16)
            bias = jnp.concatenate([bias] * 10, axis=0)
            w_here = w_expand_ref[:, at]
            grown = jnp.dot(normed_ref[...], w_here, preferred_element_type=F32).astype(BF16)
            for r in range(10):
                g = double_gelu(grown[160 * r : 160 * (r + 1)] + bias)
                if r == 0:
                    g = g * keep_top
                if r == 9:
                    g = g * keep_bottom
                if on_side:
                    keep = keep_left if block == 0 else keep_right
                    if block == 0:
                        g = jnp.concatenate([(g[:16] * keep.astype(BF16)), g[16:]], axis=0)
                    else:
                        g = jnp.concatenate([g[:144], (g[144:] * keep.astype(BF16))], axis=0)
                grown_ref[r] = g.reshape(10, 16, SLICE)
            for half in range(SLICE // 128):
                lanes = slice(128 * half, 128 * (half + 1))
                there = pl.ds(pl.multiple_of(s * SLICE + 128 * half, 128), 128)
                taps = [
                    jnp.broadcast_to(0.5 * depth_ref[i // 3, i % 3 : i % 3 + 1, there], (16, 128)).astype(BF16)
                    for i in range(9)
                ]
                depth_bias = jnp.broadcast_to(b_depth_ref[:, there], (16, 128)).astype(BF16)
                for c in range(8):
                    near = [[grown_ref[r, c + dj, :, lanes] for r in range(10)] for dj in range(3)]
                    for r in range(8):
                        p = [
                            taps[dj] * near[dj][r]
                            + taps[3 + dj] * near[dj][r + 1]
                            + taps[6 + dj] * near[dj][r + 2]
                            for dj in range(3)
                        ]
                        total = (p[0] + p[1]) + (p[2] + depth_bias)
                        filtered_ref[r, c, :, lanes] = double_gelu(total)
            acc_ref[...] += jnp.dot(
                filtered_ref[...].reshape(1024, SLICE),
                w_project_ref[at, :] * jnp.asarray(0.5, BF16),
                preferred_element_type=F32,
            )

        def two_slices(s, carry):
            channels(2 * s)
            channels(2 * s + 1)
            return carry

        lax.fori_loop(0, WIDE // SLICE // 2, two_slices, 0)
        mixed = acc_ref[...].astype(BF16)
        turned = [
            jnp.dot(swap, mixed[256 * i : 256 * (i + 1)], preferred_element_type=F32) for i in range(4)
        ]
        tokens = jnp.concatenate(
            [turned[i][16 * k : 16 * k + 16] for k in range(16) for i in range(4)], axis=0
        )
        halves.append(tokens)
    done = attend(
        jnp.concatenate(halves, axis=0), gain2_ref[...], w_qkv_ref[...], w_out_ref[...]
    )
    for k in range(16):
        both = jnp.concatenate(
            [done[1024 * h + 64 * k : 1024 * h + 64 * k + 64].reshape(8, 8, WIDTH) for h in range(2)], axis=1
        )
        out_ref[8 * (k % 8) : 8 * (k % 8) + 8, k // 8] = both.astype(BF16)


def local_stage(blocks, field, north, south, side, weights):
    vmem = pl.BlockSpec(memory_space=pltpu.VMEM)
    arrays = (field, north, south) + ((side,) if 0 in blocks else ()) + weights
    return pl.pallas_call(
        functools.partial(local_kernel, blocks),
        in_specs=[vmem] * len(arrays),
        out_specs=vmem,
        out_shape=jax.ShapeDtypeStruct((64, 2, 16, WIDTH), BF16),
        scratch_shapes=[
            pltpu.VMEM((1600, WIDTH), BF16),
            pltpu.VMEM((10, 10, 16, SLICE), BF16),
            pltpu.VMEM((8, 8, 16, SLICE), BF16),
            pltpu.VMEM((1024, WIDTH), F32),
        ],
        compiler_params=pltpu.CompilerParams(vmem_limit_bytes=VMEM_LIMIT),
        cost_estimate=pl.CostEstimate(
            flops=5_000_000_000, bytes_accessed=3_000_000, transcendentals=6_000_000
        ),
        name="local_stage",
    )(*arrays)


def grid_kernel(in_ref, gain_ref, w_qkv_ref, w_out_ref, *refs):
    out_ref = refs[-1]
    swap = swap_matrix()
    turned = []
    for c in range(4):
        block = in_ref[8 * c : 8 * c + 8].reshape(256, WIDTH)
        turned.append(jnp.dot(swap, block, preferred_element_type=F32))
    tokens = jnp.concatenate(
        [turned[c][16 * k : 16 * k + 16] for k in range(16) for c in range(4)], axis=0
    )
    done = attend(tokens, gain_ref[...], w_qkv_ref[...], w_out_ref[...]).astype(BF16)
    for c in range(4):
        block = jnp.concatenate([done[64 * k + 16 * c : 64 * k + 16 * c + 16] for k in range(16)], axis=0)
        back = jnp.dot(swap, block, preferred_element_type=F32)
        at = slice(8 * c, 8 * c + 8)
        if len(refs) == 1:
            out_ref[at] = back.astype(BF16).reshape(8, 1, 2, 16, WIDTH)
        else:
            back = back.reshape(16, 16, WIDTH)
            inner = refs[0][at].astype(F32).reshape(16, 16, WIDTH)
            rows = jnp.concatenate([back[:, :8], inner, back[:, 8:]], axis=1)
            out_ref[at] = rows.astype(BF16).reshape(8, 1, 2, COLS, WIDTH)


def grid_stage(landed, weights, inner):
    whole = lambda a: pl.BlockSpec(a.shape, lambda r: (0,) * a.ndim)
    block = lambda n: pl.BlockSpec((32, 1, 2, n, WIDTH), lambda r: (0, r, 0, 0, 0))
    more = () if inner is None else (inner,)
    columns = COLS if more else 16
    return pl.pallas_call(
        grid_kernel,
        grid=(2,),
        in_specs=[block(16)] + [whole(w) for w in weights] + [block(16)] * len(more),
        out_specs=block(columns),
        out_shape=jax.ShapeDtypeStruct((32, 2, 2, columns, WIDTH), BF16),
        compiler_params=pltpu.CompilerParams(
            dimension_semantics=("arbitrary",), vmem_limit_bytes=VMEM_LIMIT
        ),
        cost_estimate=pl.CostEstimate(
            flops=3_000_000_000, bytes_accessed=2_500_000, transcendentals=1_000_000
        ),
        name="grid_stage",
    )(landed, *weights, *more)


def shift(values, axis, step, count):
    pairs = [(i, i + step) for i in range(count) if 0 <= i + step < count]
    return lax.ppermute(values, axis, pairs)


LON = ("j", "m")


def per_device(
    field,
    norm_gain,
    expand_weight,
    expand_bias,
    depth_kernel,
    depth_bias,
    project_weight,
    block_gain,
    block_qkv,
    block_out,
    grid_gain,
    grid_qkv,
    grid_out,
):
    lat_count, lon_count = 4, 32
    north = shift(field[-1:], "lat", 1, lat_count)
    south = shift(field[:1], "lat", -1, lat_count)

    def side(at):
        return jnp.concatenate([north[:, at], field[:, at], south[:, at]], axis=0)

    left = shift(side(COLS - 1), LON, 1, lon_count)
    right = shift(side(0), LON, -1, lon_count)

    def bands(column):
        middle = column[1:129].reshape(16, 8, WIDTH).transpose(1, 0, 2)
        first = jnp.concatenate([column[None, :1], middle[7:, :15]], axis=1)
        last = jnp.concatenate([middle[:1, 1:], column[None, 129:]], axis=1)
        return jnp.concatenate([first, middle, last], axis=0)

    sides = jnp.concatenate([bands(left), bands(right)], axis=1)
    local_weights = (
        norm_gain[None],
        expand_weight,
        expand_bias[None],
        depth_kernel,
        depth_bias[None],
        project_weight,
        block_gain[None],
        block_qkv,
        block_out,
    )
    grid_weights = (grid_gain[None], grid_qkv, grid_out)
    shape = (32, 64, WIDTH)
    exchange = lambda parcels: lax.all_to_all(parcels.reshape(shape), ("lat", "j"), 0, 0, tiled=True)
    inner = local_stage((1, 2), field, north, south, None, local_weights)
    inner_landed = exchange(inner)
    sides, _ = lax.optimization_barrier((sides, inner))
    outer = local_stage((0, 3), field, north, south, sides, local_weights)
    outer, _ = lax.optimization_barrier((outer, inner_landed))
    outer_landed = exchange(outer)
    pieces = (32, 2, 2, 16, WIDTH)
    done = grid_stage(inner_landed.reshape(pieces), grid_weights, None)
    done = grid_stage(outer_landed.reshape(pieces), grid_weights, done)
    back = lax.all_to_all(done.reshape(32, 128, WIDTH), ("lat", "j"), 0, 0, tiled=True)
    return back.reshape(64, 2, COLS, WIDTH).transpose(1, 0, 2, 3).reshape(128, COLS, WIDTH)


def solution(mesh):
    inner = Mesh(mesh.devices.reshape(4, 8, 4), ("lat", "j", "m"))
    return jax.shard_map(
        per_device,
        mesh=inner,
        in_specs=(P("lat", LON, None),) + (P(),) * 12,
        out_specs=P("lat", LON, None),
        check_vma=False,
    )
```
